512 devices in a mesh: dp: 2 (over x_hi), tm: 16 (over z, x_lo), space: 16 (over y, core).
Axes of the slice: x: 4 (x_hi: 2, x_lo: 2; x = x_hi * 2 + x_lo), y: 8, z: 8, core: 2. Of those that a mesh axis runs over, the one named last changes fastest.
Arguments:
- queries: bfloat16 [4, 16, 32, 32, 1152], P('dp', 'tm', 'space'), may hold values from -6 to 6
- key_states: bfloat16 [4, 16, 32, 32, 1152], P('dp', 'tm', 'space'), may hold values from -6 to 6
- value_states: bfloat16 [4, 16, 32, 32, 1152], P('dp', 'tm', 'space'), may hold values from -6 to 6
- grad_out: bfloat16 [4, 16, 32, 32, 1152], P('dp', 'tm', 'space'), may hold values from -3 to 3
- attn_out: bfloat16 [4, 16, 32, 32, 1152], P('dp', 'tm', 'space'), may hold values from -6 to 6
- w_out: bfloat16 [1152, 1152], P('tm'), may hold values from -0.1875 to 0.1875
Outputs:
- grad_queries: bfloat16 [4, 16, 32, 32, 1152], P('dp', 'tm', 'space')
- grad_keys: bfloat16 [4, 16, 32, 32, 1152], P('dp', 'tm', 'space')
- grad_values: bfloat16 [4, 16, 32, 32, 1152], P('dp', 'tm', 'space')
- grad_w_out: float32 [1152, 1152], P('tm')
The draws below stay inside these ranges and needn't reach their ends.
All inputs are finite; a program needn't handle non-finite values.
Results may differ from the reference program's by a relative error of at most 0.02.
Values may be sent and summed in bfloat16 or wider, within the bound.
No kernel may reach another device: no remote copies, remote signals or barrier semaphores. Data moves between devices by JAX's collectives and lax.ppermute only.
A program may use at most 64 MiB of HBM per device.

```python
import math
import jax
import jax.numpy as jnp
from jax import lax

D = 1152
HEADS = 16
HD = 72
W = 32
ROWS_DEV = 2
FR_DEV = 1
VID_DEV = 2
VIDEOS = 4
FRAMES = 16
H = 32
N_DP = 2
N_TM = 16
N_SPACE = 16


def draw_queries(key, part):
    key = jax.random.fold_in(key, 1)
    base = jnp.clip(jax.random.normal(key, (VIDEOS, FRAMES, H, W, D), jnp.float32), -6.0, 6.0)
    return base.astype(jnp.bfloat16)


def draw_key_states(key, part):
    key = jax.random.fold_in(key, 2)
    base = jnp.clip(jax.random.normal(key, (VIDEOS, FRAMES, H, W, D), jnp.float32), -6.0, 6.0)
    return base.astype(jnp.bfloat16)


def with_spikes(result, key, source, target, parts, factor):
    owner, partner = [(jnp.arange(result.shape[axis_at]) // (result.shape[axis_at] // parts)).reshape([-1 if axis == axis_at else 1 for axis in range(result.ndim)]) for axis_at in (source, target)]
    chosen = jax.random.permutation(key, parts)[partner]
    strong = (owner == chosen) | (owner == (partner + parts // 2) % parts)
    return jnp.where(strong, factor * result, result)


def block_scale(key, dims, split, low, top_value):
    def one(position, parts):
        heights = jax.random.uniform(jax.random.fold_in(jax.random.fold_in(key, 6), position), (parts,), jnp.float32, low / len(split), top_value / len(split))
        return jnp.repeat(jnp.exp(heights), dims[position] // parts).reshape((-1,) + (1,) * (len(dims) - position - 1))

    loudness = one(*split[0])
    for cut in split[1:]:
        loudness = loudness * one(*cut)
    return loudness


def scatter_about(stream_key, extent, width, most, pieces=(), kind=jnp.bfloat16):
    drawn = jax.random.normal(stream_key, extent, jnp.float32) * width
    if len(pieces) > 0:
        drawn = block_scale(stream_key, extent, pieces, -0.22, 0.18) * drawn
    return jnp.clip(drawn, min=-most, max=most).astype(kind)


def heavy_noise(rng, shape, deviation, limit, pieces, heavy, kind=jnp.bfloat16):
    values = deviation * jax.random.normal(rng, shape, jnp.float32)
    if pieces:
        values = values * block_scale(rng, shape, pieces, -0.22, 0.18)
    return jnp.clip(with_spikes(values, jax.random.fold_in(rng, 3), *heavy), -limit, limit).astype(kind)


def setup_inputs(seed: int = 0) -> dict:
    splits = jax.random.split(jax.random.key(seed), 7)
    queries = draw_queries(jax.random.fold_in(splits[6], 71), 0)
    key_states = draw_key_states(jax.random.fold_in(splits[6], 71), 0)
    value_states = scatter_about(splits[2], (VIDEOS, FRAMES, H, W, D), 1.0, 6.0, ((0, 2), (1, 16), (2, 16)))
    grad_out = scatter_about(splits[3], (VIDEOS, FRAMES, H, W, D), 0.5, 3.0, ((0, 2), (1, 16), (2, 16)))
    attn_out = heavy_noise(splits[4], (VIDEOS, FRAMES, H, W, D), 1.0, 6.0, ((0, 2), (1, 16), (2, 16)), (1, 4, 16, 2.0))
    w_out = scatter_about(splits[5], (D, D), D ** -0.5, 0.1875, ((0, 16),))
    return {"queries": queries, "key_states": key_states, "value_states": value_states, "grad_out": grad_out, "attn_out": attn_out, "w_out": w_out}


def frame_backward(q_rows, k_rows, v_rows, d_rows):
    scale_factor = 1.0 / math.sqrt(q_rows.shape[-1])
    q_float = q_rows.astype(jnp.float32)
    k_float = k_rows.astype(jnp.float32)
    v_float = v_rows.astype(jnp.float32)
    d_float = d_rows.astype(jnp.float32)
    scores = jnp.einsum('xhd,yhd->hxy', q_float, k_float) * scale_factor
    highest = lax.optimization_barrier(jnp.max(scores, axis=-1, keepdims=True))
    weights = jnp.exp(scores - highest)
    probabilities = weights / lax.optimization_barrier(jnp.sum(weights, axis=-1, keepdims=True))
    rounded = probabilities.astype(jnp.bfloat16).astype(jnp.float32)
    grad_v = jnp.einsum('hxy,xhd->yhd', rounded, d_float).astype(jnp.bfloat16)
    grad_p = jnp.einsum('xhd,yhd->hxy', d_float, v_float)
    row_terms = lax.optimization_barrier(jnp.sum(probabilities * grad_p, axis=-1, keepdims=True))
    grad_s = (probabilities * (grad_p - row_terms)).astype(jnp.bfloat16).astype(jnp.float32)
    grad_q = (jnp.einsum('hxy,yhd->xhd', grad_s, k_float) * scale_factor).astype(jnp.bfloat16)
    grad_k = (jnp.einsum('hxy,xhd->yhd', grad_s, q_float) * scale_factor).astype(jnp.bfloat16)
    return (grad_q, grad_k, grad_v)

def per_frame(bundle):
    return frame_backward(bundle[0], bundle[1], bundle[2], bundle[3])

def to_blocks(array):
    split_up = array.reshape(N_DP, VID_DEV, N_TM, FR_DEV, N_SPACE, ROWS_DEV, W, D)
    moved = jnp.transpose(split_up, (0, 2, 4, 1, 3, 5, 6, 7))
    return moved.reshape(N_DP * N_TM * N_SPACE, VID_DEV * FR_DEV * ROWS_DEV * W, D)

def accumulate(total, paired):
    term = jnp.dot(paired[0].T, paired[1], preferred_element_type=jnp.float32)
    rounded_term = lax.optimization_barrier(term.astype(jnp.bfloat16)).astype(jnp.float32)
    return (total + rounded_term, None)

def reference(queries, key_states, value_states, grad_out, attn_out, w_out):
    flat_grad = grad_out.reshape(-1, D)
    head_grad = jnp.dot(flat_grad, w_out.T, preferred_element_type=jnp.float32).astype(jnp.bfloat16)
    layout = (VIDEOS * FRAMES, H * W, HEADS, HD)
    results = lax.map(per_frame, (queries.reshape(layout), key_states.reshape(layout), value_states.reshape(layout), head_grad.reshape(layout)))
    whole_shape = (VIDEOS, FRAMES, H, W, D)
    grad_queries = results[0].reshape(whole_shape)
    grad_keys = results[1].reshape(whole_shape)
    grad_values = results[2].reshape(whole_shape)
    grad_w_out, leftover = lax.scan(accumulate, jnp.zeros((D, D), jnp.float32), (to_blocks(attn_out), to_blocks(grad_out)))
    return (grad_queries, grad_keys, grad_values, grad_w_out)
```

```python
import math

import jax
import jax.numpy as jnp
from jax import lax
from jax.experimental import pallas as pl
from jax.experimental.pallas import tpu as pltpu
from jax.sharding import Mesh
from jax.sharding import PartitionSpec as P

D = 1152
HEADS = 16
HD = 72
TOKENS = 128
FRAME = 1024
HALF = 40
PIECE = 48
QUERIES = 256
SCALE = 1.0 / math.sqrt(HD)
LOG2E = math.log2(math.e)
BF16 = jnp.bfloat16
F32 = jnp.float32
SPACE = ("y", "core")


def dot(a, b, dim_a, dim_b):
    return lax.dot_general(a, b, (((dim_a,), (dim_b,)), ((), ())), preferred_element_type=F32)


def pack_kernel(q_ref, k_ref, v_ref, out_ref):
    for j, ref in enumerate((q_ref, k_ref, v_ref)):
        turned = ref[...].astype(F32).T
        for h in range(HEADS):
            out_ref[h, j] = turned[HD * h : HD * h + HD].astype(BF16)


def pack(q, k, v):
    return pl.pallas_call(
        pack_kernel,
        out_shape=jax.ShapeDtypeStruct((HEADS, 3, HD, TOKENS), BF16),
        compiler_params=pltpu.CompilerParams(vmem_limit_bytes=16 * 2**20),
        cost_estimate=pl.CostEstimate(flops=0, bytes_accessed=2 * 2**20, transcendentals=0),
    )(q, k, v)


def unpack_kernel(x_ref, q_ref, k_ref, v_ref):
    for j, ref in enumerate((q_ref, k_ref, v_ref)):
        whole = jnp.concatenate([x_ref[h, j].astype(F32) for h in range(HEADS)], axis=0)
        ref[...] = whole.T.astype(BF16)


def unpack(x):
    out = jax.ShapeDtypeStruct((TOKENS, D), BF16)
    return pl.pallas_call(
        unpack_kernel,
        out_shape=(out, out, out),
        compiler_params=pltpu.CompilerParams(vmem_limit_bytes=16 * 2**20),
        cost_estimate=pl.CostEstimate(flops=0, bytes_accessed=2 * 2**20, transcendentals=0),
    )(x)


def pair_videos(first, second):
    low = lax.broadcasted_iota(jnp.int32, first.shape, 1) < 64
    return (
        jnp.where(low, first, pltpu.roll(second, 64, 1)),
        jnp.where(low, pltpu.roll(first, 64, 1), second),
    )


def attention_kernel(qkv_ref, g_ref, out_ref, held):
    for i in range(HEADS // 2):
        lanes = slice(TOKENS * i, TOKENS * (i + 1))
        for j in range(3):
            pair = pair_videos(qkv_ref[2 * i, j].astype(F32), qkv_ref[2 * i + 1, j].astype(F32))
            held[0, j, :, lanes] = pair[0].astype(BF16)
            held[1, j, :, lanes] = pair[1].astype(BF16)
        upper, lower = g_ref[2 * i].astype(F32), g_ref[2 * i + 1].astype(F32)
        g = jnp.concatenate([upper, lower[2 * HALF - HD :]], axis=0)
        pair = pair_videos(g[:, :TOKENS], g[:, TOKENS:])
        held[0, 3, :, lanes] = pair[0].astype(BF16)
        held[1, 3, :, lanes] = pair[1].astype(BF16)
    results = []
    for video in range(2):
        k, v = held[video, 1], held[video, 2]
        grad_q = []
        grad_k = jnp.zeros((HD, FRAME), F32)
        grad_v = jnp.zeros((HD, FRAME), F32)
        for step in range(FRAME // QUERIES):
            lanes = slice(QUERIES * step, QUERIES * (step + 1))
            q, g = held[video, 0, :, lanes], held[video, 3, :, lanes]
            scores = dot(q, k, 0, 0)
            highest = jnp.max(scores, axis=1, keepdims=True)
            weights = jnp.exp2((scores - highest) * (SCALE * LOG2E))
            probabilities = weights * (1.0 / jnp.sum(weights, axis=1, keepdims=True))
            grad_p = dot(g, v, 0, 0)
            row_terms = jnp.sum(probabilities * grad_p, axis=1, keepdims=True)
            grad_s = (probabilities * (grad_p - row_terms)).astype(BF16)
            grad_v = grad_v + dot(g, probabilities.astype(BF16), 1, 0)
            grad_k = grad_k + dot(q, grad_s, 1, 0)
            grad_q.append(dot(k, grad_s, 1, 1))
        results.append((jnp.concatenate(grad_q, axis=1) * SCALE, grad_k * SCALE, grad_v))
    for i in range(HEADS // 2):
        lanes = slice(TOKENS * i, TOKENS * (i + 1))
        for j in range(3):
            pair = pair_videos(results[0][j][:, lanes], results[1][j][:, lanes])
            out_ref[2 * i, j] = pair[0].astype(BF16)
            out_ref[2 * i + 1, j] = pair[1].astype(BF16)


def attention(qkv, g):
    return pl.pallas_call(
        attention_kernel,
        out_shape=jax.ShapeDtypeStruct((HEADS, 3, HD, TOKENS), BF16),
        scratch_shapes=[pltpu.VMEM((2, 4, HD, FRAME), BF16)],
        compiler_params=pltpu.CompilerParams(vmem_limit_bytes=48 * 2**20),
        cost_estimate=pl.CostEstimate(
            flops=2 * 2 * 5 * FRAME * FRAME * 256,
            bytes_accessed=3 * 2**20,
            transcendentals=2 * FRAME * FRAME,
        ),
    )(qkv, g)


def exchange(x, axis):
    return lax.ppermute(x, axis, [(0, 1), (1, 0)])


def all_to_all(x, axis):
    return lax.all_to_all(x, axis, split_axis=0, concat_axis=0, tiled=True)


def interleave_kernel(after_ref, even_ref, odd_ref, out_ref):
    for i in range(HEADS // 2):
        out_ref[2 * i] = even_ref[i]
        out_ref[2 * i + 1] = odd_ref[i]


def interleave_after(after, even, odd):
    vmem = pl.BlockSpec(memory_space=pltpu.VMEM)
    return pl.pallas_call(
        interleave_kernel,
        out_shape=jax.ShapeDtypeStruct((HEADS, HALF, 2 * TOKENS), BF16),
        in_specs=[pl.BlockSpec(memory_space=pl.ANY), vmem, vmem],
        compiler_params=pltpu.CompilerParams(vmem_limit_bytes=8 * 2**20),
        cost_estimate=pl.CostEstimate(flops=0, bytes_accessed=2**20, transcendentals=0),
    )(after, even, odd)


def head_cotangents(grad_out, w_rows, after):
    parity = lax.axis_index("xl")
    gathered = lax.all_gather(w_rows, "z", axis=0, tiled=True)
    tokens = lax.all_gather(grad_out, ("xl", "core"), axis=0, tiled=True)
    both = dot(gathered, tokens, 1, 1).astype(BF16)
    own = lax.dynamic_slice_in_dim(both, 2 * TOKENS * parity, 2 * TOKENS, axis=1)
    other = lax.dynamic_slice_in_dim(both, 2 * TOKENS * (1 - parity), 2 * TOKENS, axis=1)
    arrived = exchange(other, "xl").reshape(HEADS // 2, HALF, 2 * TOKENS)
    own = own.reshape(HEADS // 2, HALF, 2 * TOKENS)
    even = jnp.where(parity == 0, own, arrived)
    odd = jnp.where(parity == 0, arrived, own)
    return interleave_after(after, even, odd)


def along_x(x, flip_dp, flip_xl):
    pairs = [(2 * a + b, 2 * (a ^ flip_dp) + (b ^ flip_xl)) for a in (0, 1) for b in (0, 1)]
    return lax.ppermute(x, ("dp", "xl"), pairs)


def add_kernel(after_ref, a_ref, b_ref, c_ref, d_ref, out_ref):
    total = a_ref[...].astype(F32) + b_ref[...].astype(F32)
    total = total + c_ref[...].astype(F32) + d_ref[...].astype(F32)
    out_ref[...] = total.astype(BF16)


def add_after(after, parts):
    vmem = pl.BlockSpec(memory_space=pltpu.VMEM)
    return pl.pallas_call(
        add_kernel,
        out_shape=jax.ShapeDtypeStruct(parts[0].shape, BF16),
        in_specs=[pl.BlockSpec(memory_space=pl.ANY)] + [vmem] * 4,
        compiler_params=pltpu.CompilerParams(vmem_limit_bytes=8 * 2**20),
        cost_estimate=pl.CostEstimate(flops=0, bytes_accessed=2**20, transcendentals=0),
    )(after, *parts)


def sum_along_x(rows, after):
    parity = lax.axis_index("xl")
    own = lax.dynamic_slice_in_dim(rows, HD * parity, HD, axis=0)
    other = lax.dynamic_slice_in_dim(rows, HD * (1 - parity), HD, axis=0)
    parts = (own, along_x(other, 0, 1), along_x(own, 1, 0), along_x(other, 1, 1))
    return add_after(after, parts)


def to_pieces(x):
    tiles = x.reshape(9, 8, 9, 128).transpose(0, 2, 1, 3).reshape(81, 8, 128)
    return jnp.pad(tiles, ((0, 15), (0, 0), (0, 0))).reshape(HEADS, PIECE, 128)


def from_pieces(x):
    tiles = x.reshape(96, 8, 128)[:81].reshape(9, 9, 8, 128)
    return tiles.transpose(0, 2, 1, 3).reshape(HD, D)


def shards(queries, key_states, value_states, grad_out, attn_out, w_out):
    local_shape = queries.shape
    q, k, v, grad_out, attn_out = (
        a.reshape(TOKENS, D) for a in (queries, key_states, value_states, grad_out, attn_out)
    )
    core = lax.axis_index("core")
    term = dot(attn_out, grad_out, 0, 0).astype(BF16)
    rows = lax.psum_scatter(term, "z", scatter_dimension=0, tiled=True)
    w_rows = lax.dynamic_slice_in_dim(w_out, (HD - HALF) * core, HALF, axis=0)
    packed, w_rows = lax.optimization_barrier((pack(q, k, v), w_rows))
    qkv = all_to_all(packed, SPACE)
    g = head_cotangents(grad_out, w_rows, qkv)
    g, rows = lax.optimization_barrier((g, rows))
    g = all_to_all(g, SPACE)
    pieces = all_to_all(to_pieces(sum_along_x(rows, g)), SPACE)
    piece = jnp.sum(pieces.astype(F32), axis=0, keepdims=True).astype(BF16)
    sent = jnp.concatenate(
        [
            attention(qkv, g).reshape(HEADS, 3 * HD, 128),
            jnp.broadcast_to(piece, (HEADS, PIECE, 128)),
        ],
        axis=1,
    )
    arrived = all_to_all(sent, SPACE)
    grads = unpack(arrived[:, : 3 * HD].reshape(HEADS, 3, HD, TOKENS))
    grad_w_out = from_pieces(arrived[:, 3 * HD :].astype(F32))
    return tuple(a.reshape(local_shape) for a in grads) + (grad_w_out,)


def solution(mesh):
    fine = Mesh(mesh.devices.reshape(2, 8, 2, 8, 2), ("dp", "z", "xl", "y", "core"))
    tokens = P("dp", ("z", "xl"), ("y", "core"), None, None)
    rows = P(("z", "xl"), None)
    return jax.shard_map(
        shards,
        mesh=fine,
        in_specs=(tokens,) * 5 + (rows,),
        out_specs=(tokens,) * 3 + (rows,),
        check_vma=False,
    )
```

```python
import functools
import math

import jax
import jax.numpy as jnp
from jax import lax
from jax.experimental import pallas as pl
from jax.experimental.pallas import tpu as pltpu
from jax.sharding import Mesh
from jax.sharding import PartitionSpec as P

D = 1152
HEADS = 16
HD = 72
TOKENS = 128
FRAME = 1024
HALF = 40
PIECE = 24
RING = 8
QUERIES = 256
SCALE = 1.0 / math.sqrt(HD)
LOG2E = math.log2(math.e)
BF16 = jnp.bfloat16
F32 = jnp.float32
SPACE = ("y", "core")


def dot(a, b, dim_a, dim_b):
    return lax.dot_general(a, b, (((dim_a,), (dim_b,)), ((), ())), preferred_element_type=F32)


def pack_kernel(q_ref, k_ref, v_ref, out_ref):
    for j, ref in enumerate((q_ref, k_ref, v_ref)):
        turned = ref[...].astype(F32).T
        for h in range(HEADS):
            out_ref[h, j] = turned[HD * h : HD * h + HD].astype(BF16)


def pack(q, k, v):
    return pl.pallas_call(
        pack_kernel,
        out_shape=jax.ShapeDtypeStruct((HEADS, 3, HD, TOKENS), BF16),
        compiler_params=pltpu.CompilerParams(vmem_limit_bytes=16 * 2**20),
        cost_estimate=pl.CostEstimate(flops=0, bytes_accessed=2 * 2**20, transcendentals=0),
    )(q, k, v)


def unpack_kernel(x_ref, q_ref, k_ref, v_ref):
    for j, ref in enumerate((q_ref, k_ref, v_ref)):
        whole = jnp.concatenate([x_ref[h, j].astype(F32) for h in range(HEADS)], axis=0)
        ref[...] = whole.T.astype(BF16)


def unpack(x):
    out = jax.ShapeDtypeStruct((TOKENS, D), BF16)
    return pl.pallas_call(
        unpack_kernel,
        out_shape=(out, out, out),
        compiler_params=pltpu.CompilerParams(vmem_limit_bytes=16 * 2**20),
        cost_estimate=pl.CostEstimate(flops=0, bytes_accessed=2 * 2**20, transcendentals=0),
    )(x)


def pair_videos(first, second):
    low = lax.broadcasted_iota(jnp.int32, first.shape, 1) < 64
    return (
        jnp.where(low, first, pltpu.roll(second, 64, 1)),
        jnp.where(low, pltpu.roll(first, 64, 1), second),
    )


def attention_kernel(qkv_ref, g_ref, out_ref, held):
    for i in range(HEADS // 2):
        lanes = slice(TOKENS * i, TOKENS * (i + 1))
        for j in range(3):
            pair = pair_videos(qkv_ref[2 * i, j].astype(F32), qkv_ref[2 * i + 1, j].astype(F32))
            held[0, j, :, lanes] = pair[0].astype(BF16)
            held[1, j, :, lanes] = pair[1].astype(BF16)
        upper, lower = g_ref[2 * i].astype(F32), g_ref[2 * i + 1].astype(F32)
        g = jnp.concatenate([upper, lower[2 * HALF - HD :]], axis=0)
        pair = pair_videos(g[:, :TOKENS], g[:, TOKENS:])
        held[0, 3, :, lanes] = pair[0].astype(BF16)
        held[1, 3, :, lanes] = pair[1].astype(BF16)
    results = []
    for video in range(2):
        k, v = held[video, 1], held[video, 2]
        grad_q = []
        grad_k = jnp.zeros((HD, FRAME), F32)
        grad_v = jnp.zeros((HD, FRAME), F32)
        for step in range(FRAME // QUERIES):
            lanes = slice(QUERIES * step, QUERIES * (step + 1))
            q, g = held[video, 0, :, lanes], held[video, 3, :, lanes]
            scores = dot(q, k, 0, 0)
            highest = jnp.max(scores, axis=1, keepdims=True)
            weights = jnp.exp2((scores - highest) * (SCALE * LOG2E))
            probabilities = weights * (1.0 / jnp.sum(weights, axis=1, keepdims=True))
            grad_p = dot(g, v, 0, 0)
            row_terms = jnp.sum(probabilities * grad_p, axis=1, keepdims=True)
            grad_s = (probabilities * (grad_p - row_terms)).astype(BF16)
            grad_v = grad_v + dot(g, probabilities.astype(BF16), 1, 0)
            grad_k = grad_k + dot(q, grad_s, 1, 0)
            grad_q.append(dot(k, grad_s, 1, 1))
        results.append((jnp.concatenate(grad_q, axis=1) * SCALE, grad_k * SCALE, grad_v))
    for i in range(HEADS // 2):
        lanes = slice(TOKENS * i, TOKENS * (i + 1))
        for j in range(3):
            pair = pair_videos(results[0][j][:, lanes], results[1][j][:, lanes])
            out_ref[2 * i, j] = pair[0].astype(BF16)
            out_ref[2 * i + 1, j] = pair[1].astype(BF16)


def attention(qkv, g):
    return pl.pallas_call(
        attention_kernel,
        out_shape=jax.ShapeDtypeStruct((HEADS, 3, HD, TOKENS), BF16),
        scratch_shapes=[pltpu.VMEM((2, 4, HD, FRAME), BF16)],
        compiler_params=pltpu.CompilerParams(vmem_limit_bytes=48 * 2**20),
        cost_estimate=pl.CostEstimate(
            flops=2 * 2 * 5 * FRAME * FRAME * 256,
            bytes_accessed=3 * 2**20,
            transcendentals=2 * FRAME * FRAME,
        ),
    )(qkv, g)


def exchange(x, axis):
    return lax.ppermute(x, axis, [(0, 1), (1, 0)])


def all_to_all(x, axis):
    return lax.all_to_all(x, axis, split_axis=0, concat_axis=0, tiled=True)


def along_z(x, apart):
    return lax.ppermute(x, "z", [(i, i ^ apart) for i in range(RING)])


def gather_weights(w_out):
    core = lax.axis_index("core")
    blocks = lax.dynamic_slice_in_dim(w_out, (HD - HALF) * core, HALF, axis=0)
    order = (0,)
    for apart in (4, 2, 1):
        blocks = jnp.concatenate([blocks, along_z(blocks, apart)], axis=0)
        order = order + tuple(r ^ apart for r in order)
    return blocks, order


def interleave_kernel(order, place_ref, after_ref, own_ref, other_ref, out_ref):
    z, parity = place_ref[0], place_ref[1]
    for i, r in enumerate(order):
        first = 2 * lax.bitwise_xor(z, r)
        out_ref[first + parity] = own_ref[i]
        out_ref[first + 1 - parity] = other_ref[i]


def interleave_after(after, own, other, order):
    vmem = pl.BlockSpec(memory_space=pltpu.VMEM)
    place = jnp.stack([lax.axis_index("z"), lax.axis_index("xl")])
    return pl.pallas_call(
        functools.partial(interleave_kernel, order),
        out_shape=jax.ShapeDtypeStruct((HEADS, HALF, 2 * TOKENS), BF16),
        in_specs=[
            pl.BlockSpec(memory_space=pltpu.SMEM),
            pl.BlockSpec(memory_space=pl.ANY),
            vmem,
            vmem,
        ],
        compiler_params=pltpu.CompilerParams(vmem_limit_bytes=8 * 2**20),
        cost_estimate=pl.CostEstimate(flops=0, bytes_accessed=2**20, transcendentals=0),
    )(place, after, own, other)


def head_cotangents(grad_out, beside, weights, order, after):
    other = dot(weights, beside, 1, 1).astype(BF16)
    arrived = exchange(other, "xl").reshape(RING, HALF, 2 * TOKENS)
    own = dot(weights, grad_out, 1, 1).astype(BF16).reshape(RING, HALF, 2 * TOKENS)
    return interleave_after(after, own, arrived, order)


def add(a, b):
    return (a.astype(F32) + b.astype(F32)).astype(BF16)


def sum_terms(attn_out, grad_out, after):
    parity, z, core = (lax.axis_index(axis) for axis in ("xl", "z", "core"))
    terms = dot(attn_out, grad_out, 0, 0).astype(BF16).reshape(RING, 2, HD, D)

    def part(which):
        at = (0, which, (HD - HALF) * core, 0)
        return lax.dynamic_slice(terms, at, (RING, 1, HALF, D)).reshape(RING, HALF, D)

    total = add(part(parity), exchange(part(1 - parity), "xl"))
    for apart in (1, 2, 4):
        mine = (z // apart) % 2
        halves = total.reshape(4 // apart, 2, HALF, D)
        arrived = along_z(lax.dynamic_index_in_dim(halves, 1 - mine, 1, keepdims=False), apart)
        kept = lax.dynamic_index_in_dim(halves, mine, 1, keepdims=False)
        total = add(kept, arrived) if apart < 4 else add_after(after, kept[0], arrived[0])
    return total


def add_kernel(after_ref, a_ref, b_ref, out_ref):
    out_ref[...] = (a_ref[...].astype(F32) + b_ref[...].astype(F32)).astype(BF16)


def add_after(after, a, b):
    vmem = pl.BlockSpec(memory_space=pltpu.VMEM)
    return pl.pallas_call(
        add_kernel,
        out_shape=jax.ShapeDtypeStruct(a.shape, BF16),
        in_specs=[pl.BlockSpec(memory_space=pl.ANY), vmem, vmem],
        compiler_params=pltpu.CompilerParams(vmem_limit_bytes=8 * 2**20),
        cost_estimate=pl.CostEstimate(flops=0, bytes_accessed=2**20, transcendentals=0),
    )(after, a, b)


def to_pieces(x):
    tiles = x.reshape(5, 8, 9, 128).transpose(0, 2, 1, 3).reshape(45, 8, 128)
    return jnp.pad(tiles, ((0, 3), (0, 0), (0, 0))).reshape(HEADS, PIECE, 128)


def from_pieces(x):
    tiles = x.transpose(1, 0, 2, 3).reshape(2, 48, 8, 128)[:, :45]
    halves = tiles.reshape(2, 5, 9, 8, 128).transpose(0, 1, 3, 2, 4).reshape(2, HALF, D)
    return jnp.concatenate([halves[0], halves[1, 2 * HALF - HD :]], axis=0)


def shards(queries, key_states, value_states, grad_out, attn_out, w_out):
    local_shape = queries.shape
    q, k, v, grad_out, attn_out = (
        a.reshape(TOKENS, D) for a in (queries, key_states, value_states, grad_out, attn_out)
    )
    weights, order = gather_weights(w_out)
    beside = exchange(grad_out, "xl")
    qkv = all_to_all(pack(q, k, v), SPACE)
    grad_out, beside, attn_out = (
        lax.all_gather(a, "core", axis=0, tiled=True) for a in (grad_out, beside, attn_out)
    )
    g = all_to_all(head_cotangents(grad_out, beside, weights, order, qkv), SPACE)
    rows = to_pieces(sum_terms(attn_out, grad_out, g))
    pieces = all_to_all(jnp.concatenate([rows, rows]), ("dp", "y", "core"))
    piece = jnp.sum(pieces.reshape(HEADS, 2, PIECE, 128).astype(F32), axis=0).astype(BF16)
    piece = piece.reshape(1, 2 * PIECE, 128)
    sent = jnp.concatenate(
        [
            attention(qkv, g).reshape(HEADS, 3 * HD, 128),
            jnp.broadcast_to(piece, (HEADS, 2 * PIECE, 128)),
        ],
        axis=1,
    )
    arrived = all_to_all(sent, SPACE)
    grads = unpack(arrived[:, : 3 * HD].reshape(HEADS, 3, HD, TOKENS))
    grad_w_out = from_pieces(arrived[:, 3 * HD :].astype(F32).reshape(HEADS, 2, PIECE, 128))
    return tuple(a.reshape(local_shape) for a in grads) + (grad_w_out,)


def solution(mesh):
    fine = Mesh(mesh.devices.reshape(2, 8, 2, 8, 2), ("dp", "z", "xl", "y", "core"))
    tokens = P("dp", ("z", "xl"), ("y", "core"), None, None)
    rows = P(("z", "xl"), None)
    return jax.shard_map(
        shards,
        mesh=fine,
        in_specs=(tokens,) * 5 + (rows,),
        out_specs=(tokens,) * 3 + (rows,),
        check_vma=False,
    )
```

```python
import functools
import math

import jax
import jax.numpy as jnp
from jax import lax
from jax.experimental import pallas as pl
from jax.experimental.pallas import tpu as pltpu
from jax.sharding import Mesh
from jax.sharding import PartitionSpec as P

D = 1152
HEADS = 16
HD = 72
TOKENS = 128
FRAME = 1024
HALF = 40
PIECE = 24
RING = 8
QUERIES = 256
SCALE = 1.0 / math.sqrt(HD)
LOG2E = math.log2(math.e)
BF16 = jnp.bfloat16
F32 = jnp.float32
SPACE = ("y", "core")


def dot(a, b, dim_a, dim_b):
    return lax.dot_general(a, b, (((dim_a,), (dim_b,)), ((), ())), preferred_element_type=F32)


def pack_kernel(q_ref, k_ref, v_ref, out_ref):
    for j, ref in enumerate((q_ref, k_ref, v_ref)):
        turned = ref[...].astype(F32).T
        for h in range(HEADS):
            out_ref[h, j] = turned[HD * h : HD * h + HD].astype(BF16)


def pack(q, k, v):
    return pl.pallas_call(
        pack_kernel,
        out_shape=jax.ShapeDtypeStruct((HEADS, 3, HD, TOKENS), BF16),
        compiler_params=pltpu.CompilerParams(vmem_limit_bytes=16 * 2**20),
        cost_estimate=pl.CostEstimate(flops=0, bytes_accessed=2 * 2**20, transcendentals=0),
    )(q, k, v)


def unpack_kernel(x_ref, q_ref, k_ref, v_ref):
    for j, ref in enumerate((q_ref, k_ref, v_ref)):
        whole = jnp.concatenate([x_ref[h, j].astype(F32) for h in range(HEADS)], axis=0)
        ref[...] = whole.T.astype(BF16)


def unpack(x):
    out = jax.ShapeDtypeStruct((TOKENS, D), BF16)
    return pl.pallas_call(
        unpack_kernel,
        out_shape=(out, out, out),
        compiler_params=pltpu.CompilerParams(vmem_limit_bytes=16 * 2**20),
        cost_estimate=pl.CostEstimate(flops=0, bytes_accessed=2 * 2**20, transcendentals=0),
    )(x)


def pair_videos(first, second):
    low = lax.broadcasted_iota(jnp.int32, first.shape, 1) < 64
    return (
        jnp.where(low, first, pltpu.roll(second, 64, 1)),
        jnp.where(low, pltpu.roll(first, 64, 1), second),
    )


def attention_kernel(qkv_ref, g_ref, out_ref, held):
    for i in range(HEADS // 2):
        lanes = slice(TOKENS * i, TOKENS * (i + 1))
        for j in range(3):
            pair = pair_videos(qkv_ref[2 * i, j].astype(F32), qkv_ref[2 * i + 1, j].astype(F32))
            held[0, j, :, lanes] = pair[0].astype(BF16)
            held[1, j, :, lanes] = pair[1].astype(BF16)
        upper, lower = g_ref[2 * i].astype(F32), g_ref[2 * i + 1].astype(F32)
        g = jnp.concatenate([upper, lower[2 * HALF - HD :]], axis=0)
        pair = pair_videos(g[:, :TOKENS], g[:, TOKENS:])
        held[0, 3, :, lanes] = pair[0].astype(BF16)
        held[1, 3, :, lanes] = pair[1].astype(BF16)
    results = []
    for video in range(2):
        k, v = held[video, 1], held[video, 2]
        grad_q = []
        grad_k = jnp.zeros((HD, FRAME), F32)
        grad_v = jnp.zeros((HD, FRAME), F32)
        for step in range(FRAME // QUERIES):
            lanes = slice(QUERIES * step, QUERIES * (step + 1))
            q, g = held[video, 0, :, lanes], held[video, 3, :, lanes]
            scores = dot(q, k, 0, 0)
            highest = jnp.max(scores, axis=1, keepdims=True)
            weights = jnp.exp2((scores - highest) * (SCALE * LOG2E))
            probabilities = weights * (1.0 / jnp.sum(weights, axis=1, keepdims=True))
            grad_p = dot(g, v, 0, 0)
            row_terms = jnp.sum(probabilities * grad_p, axis=1, keepdims=True)
            grad_s = (probabilities * (grad_p - row_terms)).astype(BF16)
            grad_v = grad_v + dot(g, probabilities.astype(BF16), 1, 0)
            grad_k = grad_k + dot(q, grad_s, 1, 0)
            grad_q.append(dot(k, grad_s, 1, 1))
        results.append((jnp.concatenate(grad_q, axis=1) * SCALE, grad_k * SCALE, grad_v))
    for i in range(HEADS // 2):
        lanes = slice(TOKENS * i, TOKENS * (i + 1))
        for j in range(3):
            pair = pair_videos(results[0][j][:, lanes], results[1][j][:, lanes])
            out_ref[2 * i, j] = pair[0].astype(BF16)
            out_ref[2 * i + 1, j] = pair[1].astype(BF16)


def attention(qkv, g):
    return pl.pallas_call(
        attention_kernel,
        out_shape=jax.ShapeDtypeStruct((HEADS, 3, HD, TOKENS), BF16),
        scratch_shapes=[pltpu.VMEM((2, 4, HD, FRAME), BF16)],
        compiler_params=pltpu.CompilerParams(vmem_limit_bytes=48 * 2**20),
        cost_estimate=pl.CostEstimate(
            flops=2 * 2 * 5 * FRAME * FRAME * 256,
            bytes_accessed=3 * 2**20,
            transcendentals=2 * FRAME * FRAME,
        ),
    )(qkv, g)


def exchange(x, axis):
    return lax.ppermute(x, axis, [(0, 1), (1, 0)])


def all_to_all(x, axis):
    return lax.all_to_all(x, axis, split_axis=0, concat_axis=0, tiled=True)


def along_z(x, apart):
    return lax.ppermute(x, "z", [(i, i ^ apart) for i in range(RING)])


def gather_weights(w_out):
    core = lax.axis_index("core")
    blocks = lax.dynamic_slice_in_dim(w_out, (HD - HALF) * core, HALF, axis=0)
    order = (0,)
    for apart in (4, 2, 1):
        blocks = jnp.concatenate([blocks, along_z(blocks, apart)], axis=0)
        order = order + tuple(r ^ apart for r in order)
    return blocks, order


def interleave_kernel(order, place_ref, after_ref, own_ref, other_ref, out_ref):
    z, parity = place_ref[0], place_ref[1]
    for i, r in enumerate(order):
        first = 2 * lax.bitwise_xor(z, r)
        out_ref[first + parity] = own_ref[i]
        out_ref[first + 1 - parity] = other_ref[i]


def interleave_after(after, own, other, order):
    vmem = pl.BlockSpec(memory_space=pltpu.VMEM)
    place = jnp.stack([lax.axis_index("z"), lax.axis_index("xl")])
    return pl.pallas_call(
        functools.partial(interleave_kernel, order),
        out_shape=jax.ShapeDtypeStruct((HEADS, HALF, 2 * TOKENS), BF16),
        in_specs=[
            pl.BlockSpec(memory_space=pltpu.SMEM),
            pl.BlockSpec(memory_space=pl.ANY),
            vmem,
            vmem,
        ],
        compiler_params=pltpu.CompilerParams(vmem_limit_bytes=8 * 2**20),
        cost_estimate=pl.CostEstimate(flops=0, bytes_accessed=2**20, transcendentals=0),
    )(place, after, own, other)


def head_cotangents(grad_out, beside, weights, order, after):
    other = dot(weights, beside, 1, 1).astype(BF16)
    arrived = exchange(other, "xl").reshape(RING, HALF, 2 * TOKENS)
    own = dot(weights, grad_out, 1, 1).astype(BF16).reshape(RING, HALF, 2 * TOKENS)
    return interleave_after(after, own, arrived, order)


def add(a, b):
    return (a.astype(F32) + b.astype(F32)).astype(BF16)


def term_kernel(place_ref, a_ref, g_ref, own_ref, other_ref, turned):
    turned[...] = a_ref[...].astype(F32).T
    rows = []
    for j in range(2):
        for i in range(RING):
            first = pl.multiple_of(2 * HD * i + place_ref[j], 8)
            rows.append(turned[pl.ds(first, HALF), :])
    result = dot(jnp.concatenate(rows, axis=0).astype(BF16), g_ref[...], 1, 0)
    for i in range(RING):
        own_ref[i] = result[HALF * i : HALF * (i + 1)].astype(BF16)
        other_ref[i] = result[HALF * (RING + i) : HALF * (RING + i + 1)].astype(BF16)


def terms(attn_out, grad_out):
    parity, core = lax.axis_index("xl"), lax.axis_index("core")
    place = jnp.stack([parity, 1 - parity]) * HD + (HD - HALF) * core
    vmem = pl.BlockSpec(memory_space=pltpu.VMEM)
    out = jax.ShapeDtypeStruct((RING, HALF, D), BF16)
    return pl.pallas_call(
        term_kernel,
        out_shape=(out, out),
        in_specs=[pl.BlockSpec(memory_space=pltpu.SMEM), vmem, vmem],
        scratch_shapes=[pltpu.VMEM((D, 2 * TOKENS), F32)],
        compiler_params=pltpu.CompilerParams(vmem_limit_bytes=24 * 2**20),
        cost_estimate=pl.CostEstimate(
            flops=4 * RING * HALF * D * 2 * TOKENS, bytes_accessed=3 * 2**20, transcendentals=0
        ),
    )(place, attn_out, grad_out)


def sum_terms(attn_out, grad_out, after):
    z = lax.axis_index("z")
    own, other = terms(attn_out, grad_out)
    total = add(own, exchange(other, "xl"))
    for apart in (1, 2, 4):
        mine = (z // apart) % 2
        halves = total.reshape(4 // apart, 2, HALF, D)
        arrived = along_z(lax.dynamic_index_in_dim(halves, 1 - mine, 1, keepdims=False), apart)
        kept = lax.dynamic_index_in_dim(halves, mine, 1, keepdims=False)
        total = add(kept, arrived) if apart < 4 else add_after(after, kept[0], arrived[0])
    return total


def add_kernel(after_ref, a_ref, b_ref, out_ref):
    out_ref[...] = (a_ref[...].astype(F32) + b_ref[...].astype(F32)).astype(BF16)


def add_after(after, a, b):
    vmem = pl.BlockSpec(memory_space=pltpu.VMEM)
    return pl.pallas_call(
        add_kernel,
        out_shape=jax.ShapeDtypeStruct(a.shape, BF16),
        in_specs=[pl.BlockSpec(memory_space=pl.ANY), vmem, vmem],
        compiler_params=pltpu.CompilerParams(vmem_limit_bytes=8 * 2**20),
        cost_estimate=pl.CostEstimate(flops=0, bytes_accessed=2**20, transcendentals=0),
    )(after, a, b)


def to_pieces(x):
    tiles = x.reshape(5, 8, 9, 128).transpose(0, 2, 1, 3).reshape(45, 8, 128)
    return jnp.pad(tiles, ((0, 3), (0, 0), (0, 0))).reshape(HEADS, PIECE, 128)


def from_pieces(x):
    tiles = x.transpose(1, 0, 2, 3).reshape(2, 48, 8, 128)[:, :45]
    halves = tiles.reshape(2, 5, 9, 8, 128).transpose(0, 1, 3, 2, 4).reshape(2, HALF, D)
    return jnp.concatenate([halves[0], halves[1, 2 * HALF - HD :]], axis=0)


def shards(queries, key_states, value_states, grad_out, attn_out, w_out):
    local_shape = queries.shape
    q, k, v, grad_out, attn_out = (
        a.reshape(TOKENS, D) for a in (queries, key_states, value_states, grad_out, attn_out)
    )
    weights, order = gather_weights(w_out)
    beside = exchange(grad_out, "xl")
    qkv = all_to_all(pack(q, k, v), SPACE)
    grad_out, beside, attn_out = (
        lax.all_gather(a, "core", axis=0, tiled=True) for a in (grad_out, beside, attn_out)
    )
    g = all_to_all(head_cotangents(grad_out, beside, weights, order, qkv), SPACE)
    rows = to_pieces(sum_terms(attn_out, grad_out, g))
    pieces = all_to_all(jnp.concatenate([rows, rows]), ("dp", "y", "core"))
    piece = jnp.sum(pieces.reshape(HEADS, 2, PIECE, 128).astype(F32), axis=0).astype(BF16)
    piece = piece.reshape(1, 2 * PIECE, 128)
    sent = jnp.concatenate(
        [
            attention(qkv, g).reshape(HEADS, 3 * HD, 128),
            jnp.broadcast_to(piece, (HEADS, 2 * PIECE, 128)),
        ],
        axis=1,
    )
    arrived = all_to_all(sent, SPACE)
    grads = unpack(arrived[:, : 3 * HD].reshape(HEADS, 3, HD, TOKENS))
    grad_w_out = from_pieces(arrived[:, 3 * HD :].astype(F32).reshape(HEADS, 2, PIECE, 128))
    return tuple(a.reshape(local_shape) for a in grads) + (grad_w_out,)


def solution(mesh):
    fine = Mesh(mesh.devices.reshape(2, 8, 2, 8, 2), ("dp", "z", "xl", "y", "core"))
    tokens = P("dp", ("z", "xl"), ("y", "core"), None, None)
    rows = P(("z", "xl"), None)
    return jax.shard_map(
        shards,
        mesh=fine,
        in_specs=(tokens,) * 5 + (rows,),
        out_specs=(tokens,) * 3 + (rows,),
        check_vma=False,
    )
```

```python
import functools
import math

import jax
import jax.numpy as jnp
from jax import lax
from jax.experimental import pallas as pl
from jax.experimental.pallas import tpu as pltpu
from jax.sharding import Mesh
from jax.sharding import PartitionSpec as P

D = 1152
HEADS = 16
HD = 72
TOKENS = 128
FRAME = 1024
HALF = 40
PIECE = 24
RING = 8
QUERIES = 256
SCALE = 1.0 / math.sqrt(HD)
LOG2E = math.log2(math.e)
BF16 = jnp.bfloat16
F32 = jnp.float32
SPACE = ("y", "core")


def dot(a, b, dim_a, dim_b):
    return lax.dot_general(a, b, (((dim_a,), (dim_b,)), ((), ())), preferred_element_type=F32)


def pack_kernel(q_ref, k_ref, v_ref, out_ref):
    for j, ref in enumerate((q_ref, k_ref, v_ref)):
        turned = ref[...].astype(F32).T
        for h in range(HEADS):
            out_ref[h, j] = turned[HD * h : HD * h + HD].astype(BF16)


def pack(q, k, v):
    return pl.pallas_call(
        pack_kernel,
        out_shape=jax.ShapeDtypeStruct((HEADS, 3, HD, TOKENS), BF16),
        compiler_params=pltpu.CompilerParams(vmem_limit_bytes=16 * 2**20),
        cost_estimate=pl.CostEstimate(flops=0, bytes_accessed=2 * 2**20, transcendentals=0),
    )(q, k, v)


def unpack_kernel(x_ref, q_ref, k_ref, v_ref):
    for j, ref in enumerate((q_ref, k_ref, v_ref)):
        whole = jnp.concatenate([x_ref[h, j].astype(F32) for h in range(HEADS)], axis=0)
        ref[...] = whole.T.astype(BF16)


def unpack(x):
    out = jax.ShapeDtypeStruct((TOKENS, D), BF16)
    return pl.pallas_call(
        unpack_kernel,
        out_shape=(out, out, out),
        compiler_params=pltpu.CompilerParams(vmem_limit_bytes=16 * 2**20),
        cost_estimate=pl.CostEstimate(flops=0, bytes_accessed=2 * 2**20, transcendentals=0),
    )(x)


def pair_videos(first, second):
    low = lax.broadcasted_iota(jnp.int32, first.shape, 1) < 64
    return (
        jnp.where(low, first, pltpu.roll(second, 64, 1)),
        jnp.where(low, pltpu.roll(first, 64, 1), second),
    )


def attention_kernel(qkv_ref, g_ref, out_ref, held):
    for i in range(HEADS // 2):
        lanes = slice(TOKENS * i, TOKENS * (i + 1))
        for j in range(3):
            pair = pair_videos(qkv_ref[2 * i, j].astype(F32), qkv_ref[2 * i + 1, j].astype(F32))
            held[0, j, :, lanes] = pair[0].astype(BF16)
            held[1, j, :, lanes] = pair[1].astype(BF16)
        upper, lower = g_ref[2 * i].astype(F32), g_ref[2 * i + 1].astype(F32)
        g = jnp.concatenate([upper, lower[2 * HALF - HD :]], axis=0)
        pair = pair_videos(g[:, :TOKENS], g[:, TOKENS:])
        held[0, 3, :, lanes] = pair[0].astype(BF16)
        held[1, 3, :, lanes] = pair[1].astype(BF16)
    results = []
    for video in range(2):
        k, v = held[video, 1], held[video, 2]
        grad_q = []
        grad_k = jnp.zeros((HD, FRAME), F32)
        grad_v = jnp.zeros((HD, FRAME), F32)
        for step in range(FRAME // QUERIES):
            lanes = slice(QUERIES * step, QUERIES * (step + 1))
            q, g = held[video, 0, :, lanes], held[video, 3, :, lanes]
            scores = dot(q, k, 0, 0)
            highest = jnp.max(scores, axis=1, keepdims=True)
            weights = jnp.exp2((scores - highest) * (SCALE * LOG2E))
            probabilities = weights * (1.0 / jnp.sum(weights, axis=1, keepdims=True))
            grad_p = dot(g, v, 0, 0)
            row_terms = jnp.sum(probabilities * grad_p, axis=1, keepdims=True)
            grad_s = (probabilities * (grad_p - row_terms)).astype(BF16)
            grad_v = grad_v + dot(g, probabilities.astype(BF16), 1, 0)
            grad_k = grad_k + dot(q, grad_s, 1, 0)
            grad_q.append(dot(k, grad_s, 1, 1))
        results.append((jnp.concatenate(grad_q, axis=1) * SCALE, grad_k * SCALE, grad_v))
    for i in range(HEADS // 2):
        lanes = slice(TOKENS * i, TOKENS * (i + 1))
        for j in range(3):
            pair = pair_videos(results[0][j][:, lanes], results[1][j][:, lanes])
            out_ref[2 * i, j] = pair[0].astype(BF16)
            out_ref[2 * i + 1, j] = pair[1].astype(BF16)


def attention(qkv, g):
    return pl.pallas_call(
        attention_kernel,
        out_shape=jax.ShapeDtypeStruct((HEADS, 3, HD, TOKENS), BF16),
        scratch_shapes=[pltpu.VMEM((2, 4, HD, FRAME), BF16)],
        compiler_params=pltpu.CompilerParams(vmem_limit_bytes=48 * 2**20),
        cost_estimate=pl.CostEstimate(
            flops=2 * 2 * 5 * FRAME * FRAME * 256,
            bytes_accessed=3 * 2**20,
            transcendentals=2 * FRAME * FRAME,
        ),
    )(qkv, g)


def exchange(x, axis):
    return lax.ppermute(x, axis, [(0, 1), (1, 0)])


def all_to_all(x, axis):
    return lax.all_to_all(x, axis, split_axis=0, concat_axis=0, tiled=True)


def along_z(x, apart):
    return lax.ppermute(x, "z", [(i, i ^ apart) for i in range(RING)])


def gather_weights(w_out):
    core = lax.axis_index("core")
    blocks = lax.dynamic_slice_in_dim(w_out, (HD - HALF) * core, HALF, axis=0)
    order = (0,)
    for apart in (4, 2, 1):
        blocks = jnp.concatenate([blocks, along_z(blocks, apart)], axis=0)
        order = order + tuple(r ^ apart for r in order)
    return blocks, order


def interleave_kernel(order, place_ref, after_ref, own_ref, other_ref, out_ref):
    z, parity = place_ref[0], place_ref[1]
    for i, r in enumerate(order):
        first = 2 * lax.bitwise_xor(z, r)
        out_ref[first + parity] = own_ref[i]
        out_ref[first + 1 - parity] = other_ref[i]


def interleave_after(after, own, other, order):
    vmem = pl.BlockSpec(memory_space=pltpu.VMEM)
    place = jnp.stack([lax.axis_index("z"), lax.axis_index("xl")])
    return pl.pallas_call(
        functools.partial(interleave_kernel, order),
        out_shape=jax.ShapeDtypeStruct((HEADS, HALF, 2 * TOKENS), BF16),
        in_specs=[
            pl.BlockSpec(memory_space=pltpu.SMEM),
            pl.BlockSpec(memory_space=pl.ANY),
            vmem,
            vmem,
        ],
        compiler_params=pltpu.CompilerParams(vmem_limit_bytes=8 * 2**20),
        cost_estimate=pl.CostEstimate(flops=0, bytes_accessed=2**20, transcendentals=0),
    )(place, after, own, other)


def head_cotangents(grad_out, beside, weights, order, after):
    other = dot(weights, beside, 1, 1).astype(BF16)
    arrived = exchange(other, "xl").reshape(RING, HALF, 2 * TOKENS)
    own = dot(weights, grad_out, 1, 1).astype(BF16).reshape(RING, HALF, 2 * TOKENS)
    return interleave_after(after, own, arrived, order)


def add(a, b):
    return (a.astype(F32) + b.astype(F32)).astype(BF16)


def term_kernel(place_ref, a_ref, g_ref, own_ref, other_ref, turned):
    turned[...] = a_ref[...].astype(F32).T
    rows = []
    for j in range(2):
        for i in range(RING):
            first = pl.multiple_of(2 * HD * i + place_ref[j], 8)
            rows.append(turned[pl.ds(first, HALF), :])
    result = dot(jnp.concatenate(rows, axis=0).astype(BF16), g_ref[...], 1, 0)
    for i in range(RING):
        own_ref[i] = result[HALF * i : HALF * (i + 1)].astype(BF16)
        other_ref[i] = result[HALF * (RING + i) : HALF * (RING + i + 1)].astype(BF16)


def terms(attn_out, grad_out):
    parity, core = lax.axis_index("xl"), lax.axis_index("core")
    place = jnp.stack([parity, 1 - parity]) * HD + (HD - HALF) * core
    vmem = pl.BlockSpec(memory_space=pltpu.VMEM)
    out = jax.ShapeDtypeStruct((RING, HALF, D), BF16)
    return pl.pallas_call(
        term_kernel,
        out_shape=(out, out),
        in_specs=[pl.BlockSpec(memory_space=pltpu.SMEM), vmem, vmem],
        scratch_shapes=[pltpu.VMEM((D, 2 * TOKENS), F32)],
        compiler_params=pltpu.CompilerParams(vmem_limit_bytes=12 * 2**20),
        cost_estimate=pl.CostEstimate(
            flops=4 * RING * HALF * D * 2 * TOKENS, bytes_accessed=3 * 2**20, transcendentals=0
        ),
    )(place, attn_out, grad_out)


def sum_terms(attn_out, grad_out, after):
    z = lax.axis_index("z")
    own, other = terms(attn_out, grad_out)
    total = add(own, exchange(other, "xl"))
    for apart in (1, 2, 4):
        mine = (z // apart) % 2
        halves = total.reshape(4 // apart, 2, HALF, D)
        arrived = along_z(lax.dynamic_index_in_dim(halves, 1 - mine, 1, keepdims=False), apart)
        kept = lax.dynamic_index_in_dim(halves, mine, 1, keepdims=False)
        total = add(kept, arrived) if apart < 4 else add_after(after, kept[0], arrived[0])
    return total


def add_kernel(after_ref, a_ref, b_ref, out_ref):
    out_ref[...] = (a_ref[...].astype(F32) + b_ref[...].astype(F32)).astype(BF16)


def add_after(after, a, b):
    vmem = pl.BlockSpec(memory_space=pltpu.VMEM)
    return pl.pallas_call(
        add_kernel,
        out_shape=jax.ShapeDtypeStruct(a.shape, BF16),
        in_specs=[pl.BlockSpec(memory_space=pl.ANY), vmem, vmem],
        compiler_params=pltpu.CompilerParams(vmem_limit_bytes=8 * 2**20),
        cost_estimate=pl.CostEstimate(flops=0, bytes_accessed=2**20, transcendentals=0),
    )(after, a, b)


def to_pieces(x):
    tiles = x.reshape(5, 8, 9, 128).transpose(0, 2, 1, 3).reshape(45, 8, 128)
    return jnp.pad(tiles, ((0, 3), (0, 0), (0, 0))).reshape(HEADS, PIECE, 128)


def from_pieces(x):
    tiles = x.transpose(1, 0, 2, 3).reshape(2, 48, 8, 128)[:, :45]
    halves = tiles.reshape(2, 5, 9, 8, 128).transpose(0, 1, 3, 2, 4).reshape(2, HALF, D)
    return jnp.concatenate([halves[0], halves[1, 2 * HALF - HD :]], axis=0)


def shards(queries, key_states, value_states, grad_out, attn_out, w_out):
    local_shape = queries.shape
    q, k, v, grad_out, attn_out = (
        a.reshape(TOKENS, D) for a in (queries, key_states, value_states, grad_out, attn_out)
    )
    weights, order = gather_weights(w_out)
    beside = exchange(grad_out, "xl")
    qkv = all_to_all(pack(q, k, v), SPACE)
    grad_out, beside, attn_out = (
        lax.all_gather(a, "core", axis=0, tiled=True) for a in (grad_out, beside, attn_out)
    )
    g = all_to_all(head_cotangents(grad_out, beside, weights, order, qkv), SPACE)
    rows = to_pieces(sum_terms(attn_out, grad_out, g))
    pieces = all_to_all(jnp.concatenate([rows, rows]), ("dp", "y", "core"))
    piece = jnp.sum(pieces.reshape(HEADS, 2, PIECE, 128).astype(F32), axis=0).astype(BF16)
    piece = piece.reshape(1, 2 * PIECE, 128)
    sent = jnp.concatenate(
        [
            attention(qkv, g).reshape(HEADS, 3 * HD, 128),
            jnp.broadcast_to(piece, (HEADS, 2 * PIECE, 128)),
        ],
        axis=1,
    )
    arrived = all_to_all(sent, SPACE)
    grads = unpack(arrived[:, : 3 * HD].reshape(HEADS, 3, HD, TOKENS))
    grad_w_out = from_pieces(arrived[:, 3 * HD :].astype(F32).reshape(HEADS, 2, PIECE, 128))
    return tuple(a.reshape(local_shape) for a in grads) + (grad_w_out,)


def solution(mesh):
    fine = Mesh(mesh.devices.reshape(2, 8, 2, 8, 2), ("dp", "z", "xl", "y", "core"))
    tokens = P("dp", ("z", "xl"), ("y", "core"), None, None)
    rows = P(("z", "xl"), None)
    return jax.shard_map(
        shards,
        mesh=fine,
        in_specs=(tokens,) * 5 + (rows,),
        out_specs=(tokens,) * 3 + (rows,),
        check_vma=False,
    )
```
